32 devices in a mesh: slot: 8 (over y, x, core), own: 4 (over z).
Axes of the slice: x: 2, y: 2, z: 4, core: 2. Of those that a mesh axis runs over, the one named last changes fastest.
Arguments:
- slot_grads: bfloat16 [32, 768, 2048], P(('slot', 'own')), may hold values from -6 to 6
- weights: bfloat16 [16, 768, 2048], P(None, 'slot', 'own'), may hold values from -0.21875 to 0.21875
- moment: float32 [16, 768, 2048], P(None, 'slot', 'own'), may hold values from -2 to 2
- second: float32 [16, 768, 2048], P(None, 'slot', 'own'), may hold values from 0.01 to 1
- counts_old: int32 [16], replicated, may hold values from 1 to 4, as said below
- counts_new: int32 [16], replicated, may hold values from 1 to 4, as said below
- inputs: bfloat16 [8192, 768], P(('slot', 'own')), may hold values from -6 to 6
- row_slot: int32 [8192, 1], P(('slot', 'own')), may hold values from 0 to 31; in each aligned block of 256 rows (0 to 255, 256 to 511, ...) at most 16 rows name the same one
Outputs:
- new_weights: bfloat16 [16, 768, 2048], P(None, 'slot', 'own')
- new_moment: float32 [16, 768, 2048], P(None, 'slot', 'own')
- new_second: float32 [16, 768, 2048], P(None, 'slot', 'own')
- outputs: bfloat16 [8192, 2048], P(('slot', 'own'))
The draws below stay inside these ranges and needn't reach their ends.
Inputs may be any that keep to these rules, and one draw needn't show every extreme that they name: counts_old sums to 32; some expert has 4 replicas and some has 1. counts_new sums to 32; some expert has 4 replicas and some has 1. `row_slot`: the 256 rows of one device name any one slot at most 16 times, a bound that some block reaches.
All inputs are finite; a program needn't handle non-finite values.
Results may differ from the reference program's by a relative error of at most 0.0049.
Values may be sent and summed in bfloat16 or wider, within the bound.
A program may use at most 128 MiB of HBM per device.

```python
import math
import jax
import jax.numpy as jnp
import numpy as np
from jax import lax

D = 2048
FF = 768
TOK_DEV = 256
SLOTS = 32
EXPERTS = 16
CAP = 16
TOKENS = 8192


def replica_counts(key):
    order = jax.random.permutation(key, EXPERTS)
    heavy = EXPERTS // 8
    light = EXPERTS // 4
    rest = EXPERTS - heavy - light
    swing = jax.random.randint(jax.random.fold_in(key, 7), (rest // 2,), -1, 2).astype(jnp.int32)
    ranked = jnp.concatenate([jnp.full((heavy,), 4, jnp.int32), jnp.full((light,), 1, jnp.int32), 2 + swing, 2 - swing])
    return jnp.zeros((EXPERTS,), jnp.int32).at[order].set(ranked)


def draw_counts_old(key, part):
    return replica_counts(jax.random.fold_in(key, 11))


def draw_counts_new(key, part):
    return replica_counts(jax.random.fold_in(key, 23))


def level_of(key, extent, pieces, least, largest):
    gain = 1.0
    for axis_at, shards_of in pieces:
        steps = jax.random.uniform(jax.random.fold_in(jax.random.fold_in(key, 6), axis_at), (shards_of,), jnp.float32, least / len(pieces), largest / len(pieces))
        gain = gain * jnp.repeat(jnp.exp(steps), extent[axis_at] // shards_of).reshape((-1,) + (1,) * (len(extent) - 1 - axis_at))
    return gain


def deal_out(stream_key, own, number, rows, count, top, most, lean):
    ranking = jax.random.permutation(stream_key, count)
    heavy_load, usual = load_shares(count, rows * top, most, lean, True), load_shares(count, rows * top, most, lean, False)
    places = jnp.arange(count)

    def named(lengths, turn):
        used = int((lengths > 0).sum())
        fixed = max(1, used // 4)
        moved = fixed + (places - fixed + turn * (used - fixed)) % max(1, count - fixed)
        return jnp.zeros((count,), jnp.int32).at[ranking[jnp.where(places < fixed, places, moved)]].set(jnp.asarray(lengths, jnp.int32))

    lengths = jnp.where(number % 4 == 0, named(heavy_load, number // 4), named(usual, number - number // 4 - 1))
    mixed = jax.random.permutation(jax.random.fold_in(own, 3), count)
    giver, sink = mixed[0:count // 2 * 2:2], mixed[1:count // 2 * 2:2]
    margin = jnp.minimum(lengths[giver] - 1, most - lengths[sink]) // 2
    margin = jnp.where((giver == ranking[0]) | (sink == ranking[0]) | (lengths[sink] == 0), 0, jnp.maximum(margin, 0))
    moved = jax.random.randint(jax.random.fold_in(own, 4), (count // 2,), 0, 1 << 20) % (margin + 1)
    lengths = lengths.at[giver].add(-moved).at[sink].add(moved)
    members = jnp.searchsorted(jnp.cumsum(lengths), jnp.arange(rows * top), side="right").astype(jnp.int32)
    table = members.reshape(top, rows).T
    table = table[jax.random.permutation(jax.random.fold_in(own, 1), rows)]
    turn = jax.random.randint(jax.random.fold_in(own, 2), (rows, 1), 0, top)
    return jnp.take_along_axis(table, (jnp.arange(top)[None, :] + turn) % top, axis=1)


def load_shares(number_of, total, most, lean, full):
    weights = [(1 << 20) // math.isqrt(rank ** lean) + 1 for rank in range(1, number_of + 1)]
    largest = most if full else min(most, max(-(-total // number_of), total * weights[0] // sum(weights)))
    least = 1 if total - largest >= number_of - 1 else 0
    given, spare = [largest] + [least] * (number_of - 1), total - largest - least * (number_of - 1)
    while spare > 0:
        movable = [i for i in range(1, number_of) if given[i] < largest] or [i for i in range(1, number_of) if given[i] < most]
        whole, budget = sum([weights[i] for i in movable]), spare
        for i in movable:
            more = min(most - given[i], max(1, budget * weights[i] // whole), spare)
            given[i] = given[i] + more
            spare = spare - more
    return np.array(given)


def normal_values(rng, extent, scale, bound, pieces=(), kind=jnp.bfloat16):
    drawn = scale * jax.random.normal(rng, extent, jnp.float32)
    if pieces:
        drawn = drawn * level_of(rng, extent, pieces, -0.22, 0.18)
    return jnp.clip(drawn, -bound, bound).astype(kind)


def setup_inputs(seed: int = 0) -> dict:
    key_of = jax.random.split(jax.random.key(seed), 9)
    slot_grads = normal_values(key_of[0], (SLOTS, FF, D), 1.0, 6.0, ((0, 32),))
    weights = normal_values(key_of[1], (EXPERTS, FF, D), FF ** -0.5, 0.21875, ((1, 8), (2, 4)))
    moment = normal_values(key_of[2], (EXPERTS, FF, D), 0.3, 2.0, ((1, 8), (2, 4)), jnp.float32)
    second = jnp.clip(jnp.exp(math.log(1.0) - 4.6051702 * jax.random.uniform(key_of[3], (EXPERTS, FF, D), jnp.float32) ** level_of(key_of[3], (EXPERTS, FF, D), ((1, 8), (2, 4)), -0.2, 0.2)), 0.01, 1.0)
    counts_old = draw_counts_old(jax.random.fold_in(key_of[8], 71), 0)
    counts_new = draw_counts_new(jax.random.fold_in(key_of[8], 71), 0)
    inputs = normal_values(key_of[6], (TOKENS, FF), 1.0, 6.0, ((0, 32),))
    row_slot_keys = jax.random.split(jax.random.fold_in(key_of[7], 1), TOKENS // TOK_DEV)
    row_slot_turns = jax.random.permutation(jax.random.fold_in(key_of[7], 3), TOKENS // TOK_DEV)
    row_slot = jax.vmap(lambda own, number: deal_out(jax.random.fold_in(key_of[7], 2), own, number, TOK_DEV, SLOTS, 1, CAP, 2))(row_slot_keys, row_slot_turns).reshape((TOKENS, 1))
    return dict(slot_grads=slot_grads, weights=weights, moment=moment, second=second, counts_old=counts_old, counts_new=counts_new, inputs=inputs, row_slot=row_slot)


def slot_table(counts, n_slots):
    bounds = jnp.cumsum(counts).astype(jnp.int32)
    slots = jnp.arange(n_slots, dtype=jnp.int32)
    return lax.optimization_barrier(jnp.sum((bounds[None, :] <= slots[:, None]).astype(jnp.int32), axis=1)).astype(jnp.int32)

def reference(slot_grads, weights, moment, second, counts_old, counts_new, inputs, row_slot):
    n_slots = slot_grads.shape[0]
    experts = weights.shape[0]
    table_old = slot_table(counts_old, n_slots)
    table_new = slot_table(counts_new, n_slots)
    grads = jax.ops.segment_sum(slot_grads.astype(jnp.float32), table_old, num_segments=experts)
    new_moment = 0.9 * moment + 0.1 * grads
    new_second = 0.95 * second + 0.05 * grads * grads
    bias_one = 1.0 - 0.9 ** 10
    bias_two = 1.0 - 0.95 ** 10
    update = 0.001 * (new_moment / bias_one) / (jnp.sqrt(new_second / bias_two) + 1e-08)
    new_weights = (weights.astype(jnp.float32) - update).astype(jnp.bfloat16)
    slots = row_slot[:, 0].astype(jnp.int32)
    order = jnp.argsort(slots, stable=True).astype(jnp.int32)
    per_slot = lax.optimization_barrier(jnp.sum((slots[None, :] == jnp.arange(n_slots, dtype=jnp.int32)[:, None]).astype(jnp.int32), axis=1))
    starts = (jnp.cumsum(per_slot) - per_slot).astype(jnp.int32)
    reach = 2 * TOK_DEV
    total_rows = inputs.shape[0]

    def one_slot(g, acc):
        offsets = jnp.arange(reach, dtype=jnp.int32)
        valid = offsets < per_slot[g]
        rows = order[jnp.minimum(starts[g] + offsets, total_rows - 1)]
        block = jnp.where(valid[:, None], inputs[rows], jnp.zeros((), jnp.bfloat16))
        result = jnp.dot(block, new_weights[table_new[g]], preferred_element_type=jnp.float32)
        result = jnp.where(valid[:, None], result, jnp.zeros((), jnp.float32))
        return acc.at[rows].add(result)
    acc = lax.fori_loop(0, n_slots, one_slot, jnp.zeros((total_rows, weights.shape[2]), jnp.float32))
    return (new_weights, new_moment, new_second, acc.astype(jnp.bfloat16))
```

```python
import jax
import jax.numpy as jnp
from jax import lax
from jax.experimental import pallas as pl
from jax.experimental.pallas import tpu as pltpu
from jax.sharding import PartitionSpec as P


def slot_table(counts, n_slots):
    bounds = jnp.cumsum(counts)
    slots = jnp.arange(n_slots, dtype=jnp.int32)
    return jnp.sum((bounds[None, :] <= slots[:, None]).astype(jnp.int32), axis=1)


def update_kernel(first, last, pieces, w, m, v, new_w, new_m, new_v):
    e = pl.program_id(0)
    grad = lax.fori_loop(
        first[e],
        last[e],
        lambda g, acc: acc + pieces[g].astype(jnp.float32),
        jnp.zeros(pieces.shape[1:], jnp.float32),
    )
    moment = 0.9 * m[0] + 0.1 * grad
    second = 0.95 * v[0] + 0.05 * grad * grad
    bias_one = 1.0 - 0.9**10
    bias_two = 1.0 - 0.95**10
    update = 0.001 * (moment / bias_one) / (jnp.sqrt(second / bias_two) + 1e-08)
    new_m[0] = moment
    new_v[0] = second
    new_w[0] = (w[0].astype(jnp.float32) - update).astype(jnp.bfloat16)


def adam(counts_old, pieces, weights, moment, second):
    experts, rows, cols = weights.shape
    last = jnp.cumsum(counts_old)
    first = last - counts_old
    one = pl.BlockSpec((1, rows, cols), lambda e, *_: (e, 0, 0))
    return pl.pallas_call(
        update_kernel,
        grid_spec=pltpu.PrefetchScalarGridSpec(
            num_scalar_prefetch=2,
            grid=(experts,),
            in_specs=[pl.BlockSpec(pieces.shape, lambda e, *_: (0, 0, 0)), one, one, one],
            out_specs=[one, one, one],
        ),
        out_shape=(
            jax.ShapeDtypeStruct(weights.shape, jnp.bfloat16),
            jax.ShapeDtypeStruct(weights.shape, jnp.float32),
            jax.ShapeDtypeStruct(weights.shape, jnp.float32),
        ),
        compiler_params=pltpu.CompilerParams(vmem_limit_bytes=40 * 1024 * 1024),
    )(first, last, pieces, weights, moment, second)


def grouped_kernel(ids, x, w, out):
    e = pl.program_id(0)

    @pl.when(e == 0)
    def _():
        out[...] = jnp.zeros_like(out)

    block = w[:, 0].reshape(x.shape[1], out.shape[1])
    produced = jnp.dot(x[...], block, preferred_element_type=jnp.float32)
    out[...] = jnp.where(ids[...] == e, produced.astype(jnp.bfloat16), out[...])


def grouped(ids, x, gathered):
    parts, experts, rows, cols = gathered.shape
    tokens, hidden = x.shape
    return pl.pallas_call(
        grouped_kernel,
        grid=(experts,),
        in_specs=[
            pl.BlockSpec((tokens, 1), lambda e: (0, 0)),
            pl.BlockSpec((tokens, hidden), lambda e: (0, 0)),
            pl.BlockSpec((parts, 1, rows, cols), lambda e: (0, e, 0, 0)),
        ],
        out_specs=pl.BlockSpec((tokens, cols), lambda e: (0, 0)),
        out_shape=jax.ShapeDtypeStruct((tokens, cols), jnp.bfloat16),
        compiler_params=pltpu.CompilerParams(vmem_limit_bytes=40 * 1024 * 1024),
    )(ids, x, gathered)


def body(slot_grads, weights, moment, second, counts_old, counts_new, inputs, row_slot):
    n_slot = lax.axis_size("slot")
    n_own = lax.axis_size("own")
    devices = n_slot * n_own
    experts, rows_here, cols_here = weights.shape
    table_new = slot_table(counts_new, devices)
    ids_here = jnp.sum(
        jnp.where(row_slot == jnp.arange(devices, dtype=jnp.int32)[None, :], table_new[None, :], 0),
        axis=1,
        keepdims=True,
    )
    ids = lax.all_gather(ids_here, "own", axis=0, tiled=True)
    x = lax.all_gather(inputs, "own", axis=0, tiled=True)
    sectioned = (
        slot_grads.reshape(n_slot, rows_here, n_own, cols_here)
        .transpose(0, 2, 1, 3)
        .reshape(devices, rows_here, cols_here)
    )
    pieces = lax.all_to_all(sectioned, ("slot", "own"), split_axis=0, concat_axis=0, tiled=True)
    new_weights, new_moment, new_second = adam(counts_old, pieces, weights, moment, second)
    gathered = lax.all_gather(new_weights, "slot", axis=0, tiled=False)
    produced = grouped(ids, x, gathered)
    outputs = lax.all_to_all(produced, "own", split_axis=0, concat_axis=1, tiled=True)
    return (new_weights, new_moment, new_second, outputs)


def solution(mesh):
    whole = P(None, "slot", "own")
    by_slot = P(("slot", "own"), None)
    return jax.shard_map(
        body,
        mesh=mesh,
        in_specs=(P(("slot", "own"), None, None), whole, whole, whole, P(), P(), by_slot, by_slot),
        out_specs=(whole, whole, whole, by_slot),
        check_vma=False,
    )
```

```python
import functools

import jax
import jax.numpy as jnp
from jax import lax
from jax.experimental import pallas as pl
from jax.experimental.pallas import tpu as pltpu
from jax.sharding import PartitionSpec as P


def slot_table(counts, n_slots):
    bounds = jnp.cumsum(counts)
    slots = jnp.arange(n_slots, dtype=jnp.int32)
    return jnp.sum((bounds[None, :] <= slots[:, None]).astype(jnp.int32), axis=1)


def update_kernel(first, last, pieces, w, m, v, new_w, new_m, new_v):
    e = pl.program_id(0)
    grad = lax.fori_loop(
        first[e],
        last[e],
        lambda g, acc: acc + pieces[g].astype(jnp.float32),
        jnp.zeros(pieces.shape[1:], jnp.float32),
    )
    moment = 0.9 * m[0] + 0.1 * grad
    second = 0.95 * v[0] + 0.05 * grad * grad
    bias_one = 1.0 - 0.9**10
    bias_two = 1.0 - 0.95**10
    update = 0.001 * (moment / bias_one) / (jnp.sqrt(second / bias_two) + 1e-08)
    new_m[0] = moment
    new_v[0] = second
    new_w[0] = (w[0].astype(jnp.float32) - update).astype(jnp.bfloat16)


def adam(counts_old, pieces, weights, moment, second):
    experts, rows, cols = weights.shape
    last = jnp.cumsum(counts_old)
    first = last - counts_old
    one = pl.BlockSpec((1, rows, cols), lambda e, *_: (e, 0, 0))
    return pl.pallas_call(
        update_kernel,
        grid_spec=pltpu.PrefetchScalarGridSpec(
            num_scalar_prefetch=2,
            grid=(experts,),
            in_specs=[pl.BlockSpec(pieces.shape, lambda e, *_: (0, 0, 0)), one, one, one],
            out_specs=[one, one, one],
        ),
        out_shape=(
            jax.ShapeDtypeStruct(weights.shape, jnp.bfloat16),
            jax.ShapeDtypeStruct(weights.shape, jnp.float32),
            jax.ShapeDtypeStruct(weights.shape, jnp.float32),
        ),
        compiler_params=pltpu.CompilerParams(vmem_limit_bytes=58 * 1024 * 1024),
    )(first, last, pieces, weights, moment, second)


CHUNKS = 8
MESH = pl.DeviceIdType.MESH


def bit_orders(n_slot):
    bits = n_slot.bit_length() - 1
    between = list(range(1, bits))
    half = len(between) // 2
    return between + [0], between[half:] + between[:half] + [0]


def flip(index, mask):
    bit = 1
    while bit <= mask:
        if mask & bit:
            index = index + bit - 2 * bit * lax.rem(lax.div(index, bit), 2)
        bit *= 2
    return index


def expert_kernel(
    n_slot, n_own, x_here, w_here, out, store, x_all, held, y, out_sems, load_sems, local_sems, x_send, x_recv, w_send, w_recv, y_send, y_recv
):
    slot = lax.axis_index("slot")
    own = lax.axis_index("own")
    tok, width = x_here.shape
    experts, rows, cols = w_here.shape
    hidden = n_slot * rows
    per = experts // CHUNKS
    orders = bit_orders(n_slot)
    bits = len(orders[0])

    partners = [(flip(slot, 1 << b), own) for b in range(bits)]
    partners += [(slot, lax.rem(own + k, n_own)) for k in range(1, n_own)]
    barrier = pltpu.get_barrier_semaphore()
    for partner in partners:
        pl.semaphore_signal(barrier, inc=1, device_id=partner, device_id_type=MESH)
    pl.semaphore_wait(barrier, len(partners))

    def step_copies(chunk, step):
        order = orders[chunk % 2]
        group = pl.ds(chunk * per, per)
        sources = [0]
        for b in order[:step]:
            sources = sources + [o ^ (1 << b) for o in sources]
        copies = []
        for i, offset in enumerate(sources):
            n = (1 << step) - 1 + i
            origin = flip(slot, offset)
            source = w_here.at[group] if offset == 0 else store.at[origin, group]
            copies.append(
                pltpu.make_async_remote_copy(
                    src_ref=source,
                    dst_ref=store.at[origin, group],
                    send_sem=w_send.at[chunk, n],
                    recv_sem=w_recv.at[chunk, n],
                    device_id=(flip(slot, 1 << order[step]), own),
                    device_id_type=MESH,
                )
            )
        return copies

    steps = [[step_copies(c, k) for k in range(bits)] for c in range(CHUNKS)]
    for c in range(CHUNKS):
        for copy in steps[c][0]:
            copy.start()
    x_copies = [
        pltpu.make_async_remote_copy(
            src_ref=x_here,
            dst_ref=x_all.at[own],
            send_sem=x_send.at[k],
            recv_sem=x_recv.at[k],
            device_id=(slot, lax.rem(own + k, n_own)),
            device_id_type=MESH,
        )
        for k in range(1, n_own)
    ]
    for copy in x_copies:
        copy.start()
    x_mine = pltpu.make_async_copy(x_here, x_all.at[own], local_sems.at[0])
    x_mine.start()
    w_mine = pltpu.make_async_copy(w_here, store.at[slot], local_sems.at[1])
    w_mine.start()
    y[...] = jnp.zeros_like(y)

    def load(chunk):
        return pltpu.make_async_copy(
            store.at[:, pl.ds(chunk * per, per)], held.at[chunk % 2], load_sems.at[chunk % 2]
        )

    def product(chunk, at, block):
        weight = held[chunk % 2, :, at].reshape(hidden, cols)
        ids = x_all[block, :, hidden : hidden + 1].astype(jnp.float32)
        number = (chunk * per + at).astype(jnp.float32)
        made = jnp.dot(x_all[block, :, :hidden], weight, preferred_element_type=jnp.float32)
        y[block] = jnp.where(ids == number, made.astype(jnp.bfloat16), y[block])

    y_copies = []

    def compute(chunk):
        load(chunk).wait()
        if chunk < CHUNKS - 1:
            def one(i, _):
                product(chunk, lax.div(i, n_own), lax.rem(i, n_own))
                return 0

            lax.fori_loop(0, per * n_own, one, 0)
            return
        for k in [n_own // 2 + j for j in range(n_own - n_own // 2)] + list(range(1, n_own // 2)) + [0]:
            block = lax.rem(own + k, n_own)

            def one(i, _):
                product(chunk, i, block)
                return 0

            lax.fori_loop(0, per, one, 0)
            target = out.at[:, pl.ds(pl.multiple_of(own * cols, cols), cols)]
            if k == 0:
                copy = pltpu.make_async_copy(y.at[block], target, out_sems.at[0])
            else:
                copy = pltpu.make_async_remote_copy(
                    src_ref=y.at[block],
                    dst_ref=target,
                    send_sem=y_send.at[k],
                    recv_sem=y_recv.at[k],
                    device_id=(slot, block),
                    device_id_type=MESH,
                )
            copy.start()
            y_copies.append(copy)

    for tick in range(CHUNKS + bits + 1):
        for k in range(bits):
            c = tick - k
            if 0 <= c < CHUNKS:
                for copy in steps[c][k]:
                    copy.wait_recv()
                if k + 1 < bits:
                    for copy in steps[c][k + 1]:
                        copy.start()
        c = tick - (bits - 1)
        if c == 0:
            w_mine.wait()
            x_mine.wait()
            for copy in x_copies:
                copy.wait_recv()
        if 0 <= c < CHUNKS:
            load(c).start()
        if 0 <= c - 1 < CHUNKS:
            compute(c - 1)
    for c in range(CHUNKS):
        for k in range(bits):
            for copy in steps[c][k]:
                copy.wait_send()
    for copy in x_copies:
        copy.wait_send()
    for copy in y_copies:
        copy.wait()


def expert_rows(n_slot, n_own, x_here, new_weights):
    tok, width = x_here.shape
    experts, rows, cols = new_weights.shape
    hbm = pl.BlockSpec(memory_space=pl.ANY)
    dma = pltpu.SemaphoreType.DMA
    return pl.pallas_call(
        functools.partial(expert_kernel, n_slot, n_own),
        in_specs=[hbm, hbm],
        out_specs=[hbm, hbm],
        out_shape=(
            jax.ShapeDtypeStruct((tok, n_own * cols), jnp.bfloat16),
            jax.ShapeDtypeStruct((n_slot, experts, rows, cols), jnp.bfloat16),
        ),
        scratch_shapes=[
            pltpu.VMEM((n_own, tok, width), jnp.bfloat16),
            pltpu.VMEM((2, n_slot, experts // CHUNKS, rows, cols), jnp.bfloat16),
            pltpu.VMEM((n_own, tok, cols), jnp.bfloat16),
            dma((1,)),
            dma((2,)),
            dma((2,)),
            dma((n_own,)),
            dma((n_own,)),
            dma((CHUNKS, n_slot - 1)),
            dma((CHUNKS, n_slot - 1)),
            dma((n_own,)),
            dma((n_own,)),
        ],
        compiler_params=pltpu.CompilerParams(
            collective_id=0, has_side_effects=True, vmem_limit_bytes=58 * 1024 * 1024
        ),
    )(x_here, new_weights)[0]


def body(slot_grads, weights, moment, second, counts_old, counts_new, inputs, row_slot):
    n_slot = lax.axis_size("slot")
    n_own = lax.axis_size("own")
    devices = n_slot * n_own
    experts, rows_here, cols_here = weights.shape
    table_new = slot_table(counts_new, devices)
    ids_here = jnp.sum(
        jnp.where(row_slot == jnp.arange(devices, dtype=jnp.int32)[None, :], table_new[None, :], 0),
        axis=1,
        keepdims=True,
    )
    marks = jnp.broadcast_to(ids_here, (inputs.shape[0], 128)).astype(jnp.bfloat16)
    x_here = jnp.concatenate([inputs, marks], axis=1)
    sectioned = (
        slot_grads.reshape(n_slot, rows_here, n_own, cols_here)
        .transpose(0, 2, 1, 3)
        .reshape(devices, rows_here, cols_here)
    )
    pieces = lax.all_to_all(sectioned, ("slot", "own"), split_axis=0, concat_axis=0, tiled=True)
    new_weights, new_moment, new_second = adam(counts_old, pieces, weights, moment, second)
    outputs = expert_rows(n_slot, n_own, x_here, new_weights)
    return (new_weights, new_moment, new_second, outputs)


def solution(mesh):
    whole = P(None, "slot", "own")
    by_slot = P(("slot", "own"), None)
    return jax.shard_map(
        body,
        mesh=mesh,
        in_specs=(P(("slot", "own"), None, None), whole, whole, whole, P(), P(), by_slot, by_slot),
        out_specs=(whole, whole, whole, by_slot),
        check_vma=False,
    )
```

```python
import functools

import jax
import jax.numpy as jnp
from jax import lax
from jax.experimental import pallas as pl
from jax.experimental.pallas import tpu as pltpu
from jax.sharding import PartitionSpec as P


def slot_table(counts, n_slots):
    bounds = jnp.cumsum(counts)
    slots = jnp.arange(n_slots, dtype=jnp.int32)
    return jnp.sum((bounds[None, :] <= slots[:, None]).astype(jnp.int32), axis=1)


def update_kernel(first, last, pieces, w, m, v, new_w, new_m, new_v):
    e = pl.program_id(0)
    grad = lax.fori_loop(
        first[e],
        last[e],
        lambda g, acc: acc + pieces[g].astype(jnp.float32),
        jnp.zeros(pieces.shape[1:], jnp.float32),
    )
    moment = 0.9 * m[0] + 0.1 * grad
    second = 0.95 * v[0] + 0.05 * grad * grad
    bias_one = 1.0 - 0.9**10
    bias_two = 1.0 - 0.95**10
    update = 0.001 * (moment / bias_one) / (jnp.sqrt(second / bias_two) + 1e-08)
    new_m[0] = moment
    new_v[0] = second
    new_w[0] = (w[0].astype(jnp.float32) - update).astype(jnp.bfloat16)


def adam(counts_old, pieces, weights, moment, second):
    experts, rows, cols = weights.shape
    last = jnp.cumsum(counts_old)
    first = last - counts_old
    one = pl.BlockSpec((1, rows, cols), lambda e, *_: (e, 0, 0))
    return pl.pallas_call(
        update_kernel,
        grid_spec=pltpu.PrefetchScalarGridSpec(
            num_scalar_prefetch=2,
            grid=(experts,),
            in_specs=[pl.BlockSpec(pieces.shape, lambda e, *_: (0, 0, 0)), one, one, one],
            out_specs=[one, one, one],
        ),
        out_shape=(
            jax.ShapeDtypeStruct(weights.shape, jnp.bfloat16),
            jax.ShapeDtypeStruct(weights.shape, jnp.float32),
            jax.ShapeDtypeStruct(weights.shape, jnp.float32),
        ),
        compiler_params=pltpu.CompilerParams(vmem_limit_bytes=58 * 1024 * 1024),
    )(first, last, pieces, weights, moment, second)


HALVES = 2
GROUPS = 4
CHUNKS = HALVES * GROUPS
LAG = 2
MESH = pl.DeviceIdType.MESH


def bit_orders(n_slot):
    bits = n_slot.bit_length() - 1
    between = list(range(1, bits))
    half = len(between) // 2
    return between + [0], between[half:] + between[:half] + [0]


def flip(index, mask):
    bit = 1
    while bit <= mask:
        if mask & bit:
            index = index + bit - 2 * bit * lax.rem(lax.div(index, bit), 2)
        bit *= 2
    return index


def expert_kernel(
    n_slot, n_own, x_here, w_here, out, store, x_all, held, y, out_sems, load_sems, local_sems, x_send, x_recv, w_send, w_recv, y_send, y_recv
):
    slot = lax.axis_index("slot")
    own = lax.axis_index("own")
    tok, width = x_here.shape
    experts, rows, cols = w_here.shape
    hidden = n_slot * rows
    per = experts // GROUPS
    wide = cols // HALVES
    orders = bit_orders(n_slot)
    bits = len(orders[0])

    partners = [(flip(slot, 1 << b), own) for b in range(bits)]
    partners += [(slot, lax.rem(own + k, n_own)) for k in range(1, n_own)]
    barrier = pltpu.get_barrier_semaphore()
    for partner in partners:
        pl.semaphore_signal(barrier, inc=1, device_id=partner, device_id_type=MESH)
    pl.semaphore_wait(barrier, len(partners))

    def step_copies(chunk, step):
        order = orders[chunk % 2]
        group = pl.ds(chunk % GROUPS * per, per)
        part = pl.ds(chunk // GROUPS * wide, wide)
        sources = [0]
        for b in order[:step]:
            sources = sources + [o ^ (1 << b) for o in sources]
        copies = []
        for i, offset in enumerate(sources):
            n = (1 << step) - 1 + i
            origin = flip(slot, offset)
            source = w_here.at[group, :, part] if offset == 0 else store.at[origin, group, :, part]
            copies.append(
                pltpu.make_async_remote_copy(
                    src_ref=source,
                    dst_ref=store.at[origin, group, :, part],
                    send_sem=w_send.at[chunk, n],
                    recv_sem=w_recv.at[chunk, n],
                    device_id=(flip(slot, 1 << order[step]), own),
                    device_id_type=MESH,
                )
            )
        return copies

    steps = [[step_copies(c, k) for k in range(bits)] for c in range(CHUNKS)]
    for c in range(CHUNKS):
        for copy in steps[c][0]:
            copy.start()
    x_copies = [
        pltpu.make_async_remote_copy(
            src_ref=x_here,
            dst_ref=x_all.at[own],
            send_sem=x_send.at[k],
            recv_sem=x_recv.at[k],
            device_id=(slot, lax.rem(own + k, n_own)),
            device_id_type=MESH,
        )
        for k in range(1, n_own)
    ]
    for copy in x_copies:
        copy.start()
    x_mine = pltpu.make_async_copy(x_here, x_all.at[own], local_sems.at[0])
    x_mine.start()
    w_mine = pltpu.make_async_copy(w_here, store.at[slot], local_sems.at[1])
    w_mine.start()
    y[...] = jnp.zeros_like(y)

    def load(chunk):
        return pltpu.make_async_copy(
            store.at[:, pl.ds(chunk % GROUPS * per, per), :, pl.ds(chunk // GROUPS * wide, wide)], held.at[chunk % 2], load_sems.at[chunk % 2]
        )

    def product(chunk, at, block):
        weight = held[chunk % 2, :, at].reshape(hidden, wide)
        ids = x_all[block, :, hidden : hidden + 1].astype(jnp.float32)
        number = (chunk % GROUPS * per + at).astype(jnp.float32)
        made = jnp.dot(x_all[block, :, :hidden], weight, preferred_element_type=jnp.float32)
        half = chunk // GROUPS
        y[half, block] = jnp.where(ids == number, made.astype(jnp.bfloat16), y[half, block])

    y_copies = []

    def compute(chunk):
        load(chunk).wait()
        half = chunk // GROUPS
        if chunk % GROUPS < GROUPS - 1:
            def one(i, _):
                product(chunk, lax.div(i, n_own), lax.rem(i, n_own))
                return 0

            lax.fori_loop(0, per * n_own, one, 0)
            return
        for k in [n_own // 2 + j for j in range(n_own - n_own // 2)] + list(range(1, n_own // 2)) + [0]:
            block = lax.rem(own + k, n_own)

            def one(i, _):
                product(chunk, i, block)
                return 0

            lax.fori_loop(0, per, one, 0)
            target = out.at[:, pl.ds(pl.multiple_of(own * cols + half * wide, wide), wide)]
            if k == 0:
                copy = pltpu.make_async_copy(y.at[half, block], target, out_sems.at[half])
            else:
                copy = pltpu.make_async_remote_copy(
                    src_ref=y.at[half, block],
                    dst_ref=target,
                    send_sem=y_send.at[half, k],
                    recv_sem=y_recv.at[half, k],
                    device_id=(slot, block),
                    device_id_type=MESH,
                )
            copy.start()
            y_copies.append(copy)

    for tick in range(CHUNKS + LAG * (bits - 1) + 1):
        for k in range(bits):
            c = tick - LAG * k
            if 0 <= c < CHUNKS:
                for copy in steps[c][k]:
                    copy.wait_recv()
                if k + 1 < bits:
                    for copy in steps[c][k + 1]:
                        copy.start()
        c = tick - LAG * (bits - 1)
        if c == 0:
            w_mine.wait()
            x_mine.wait()
            for copy in x_copies:
                copy.wait_recv()
        if 0 <= c < CHUNKS:
            load(c).start()
        if 0 <= c - 1 < CHUNKS:
            compute(c - 1)
    for c in range(CHUNKS):
        for k in range(bits):
            for copy in steps[c][k]:
                copy.wait_send()
    for copy in x_copies:
        copy.wait_send()
    for copy in y_copies:
        copy.wait()


def expert_rows(n_slot, n_own, x_here, new_weights):
    tok, width = x_here.shape
    experts, rows, cols = new_weights.shape
    hbm = pl.BlockSpec(memory_space=pl.ANY)
    dma = pltpu.SemaphoreType.DMA
    return pl.pallas_call(
        functools.partial(expert_kernel, n_slot, n_own),
        in_specs=[hbm, hbm],
        out_specs=[hbm, hbm],
        out_shape=(
            jax.ShapeDtypeStruct((tok, n_own * cols), jnp.bfloat16),
            jax.ShapeDtypeStruct((n_slot, experts, rows, cols), jnp.bfloat16),
        ),
        scratch_shapes=[
            pltpu.VMEM((n_own, tok, width), jnp.bfloat16),
            pltpu.VMEM((2, n_slot, experts // GROUPS, rows, cols // HALVES), jnp.bfloat16),
            pltpu.VMEM((HALVES, n_own, tok, cols // HALVES), jnp.bfloat16),
            dma((HALVES,)),
            dma((2,)),
            dma((2,)),
            dma((n_own,)),
            dma((n_own,)),
            dma((CHUNKS, n_slot - 1)),
            dma((CHUNKS, n_slot - 1)),
            dma((HALVES, n_own)),
            dma((HALVES, n_own)),
        ],
        compiler_params=pltpu.CompilerParams(
            collective_id=0, has_side_effects=True, vmem_limit_bytes=58 * 1024 * 1024
        ),
    )(x_here, new_weights)[0]


def body(slot_grads, weights, moment, second, counts_old, counts_new, inputs, row_slot):
    n_slot = lax.axis_size("slot")
    n_own = lax.axis_size("own")
    devices = n_slot * n_own
    experts, rows_here, cols_here = weights.shape
    table_new = slot_table(counts_new, devices)
    ids_here = jnp.sum(
        jnp.where(row_slot == jnp.arange(devices, dtype=jnp.int32)[None, :], table_new[None, :], 0),
        axis=1,
        keepdims=True,
    )
    marks = jnp.broadcast_to(ids_here, (inputs.shape[0], 128)).astype(jnp.bfloat16)
    x_here = jnp.concatenate([inputs, marks], axis=1)
    sectioned = (
        slot_grads.reshape(n_slot, rows_here, n_own, cols_here)
        .transpose(0, 2, 1, 3)
        .reshape(devices, rows_here, cols_here)
    )
    pieces = lax.all_to_all(sectioned, ("slot", "own"), split_axis=0, concat_axis=0, tiled=True)
    new_weights, new_moment, new_second = adam(counts_old, pieces, weights, moment, second)
    outputs = expert_rows(n_slot, n_own, x_here, new_weights)
    return (new_weights, new_moment, new_second, outputs)


def solution(mesh):
    whole = P(None, "slot", "own")
    by_slot = P(("slot", "own"), None)
    return jax.shard_map(
        body,
        mesh=mesh,
        in_specs=(P(("slot", "own"), None, None), whole, whole, whole, P(), P(), by_slot, by_slot),
        out_specs=(whole, whole, whole, by_slot),
        check_vma=False,
    )
```
